1024 devices in a mesh: space: 8 (over y), modej: 8 (over z), modek: 16 (over x, core).
Axes of the slice: x: 8, y: 8, z: 8, core: 2. Of those that a mesh axis runs over, the one named last changes fastest.
Arguments:
- mode_shapes: bfloat16 [3, 1024, 512], P(None, 'space', ('modej', 'modek')), may hold values from -6 to 6
- mode_grads: bfloat16 [8, 1024, 512], P(None, 'space', 'modek'), may hold values from -6 to 6
- cell_weights: float32 [1024], P('space'), may hold values from 0.005 to 0.03
Outputs:
- galerkin: bfloat16 [512, 512, 512], P('modek', ('space', 'modej'))
The draws below stay inside these ranges and needn't reach their ends.
All inputs are finite; a program needn't handle non-finite values.
Results may differ from the reference program's by a relative error of at most 0.017.
Values may be sent and summed in bfloat16 or wider, within the bound.
A program may use at most 64 MiB of HBM per device.

```python
import math
import jax
import jax.numpy as jnp
from jax import lax

MODES = 512
CELLS_DEV = 128
WINDOW = 1024
N_SPACE = 8


def block_levels(rng, extent, cuts, smallest, top_value):
    gain = 1.0
    for dim, parts in cuts:
        heights = jax.random.uniform(jax.random.fold_in(jax.random.fold_in(rng, 6), dim), (parts,), jnp.float32, smallest / len(cuts), top_value / len(cuts))
        gain = gain * jnp.repeat(jnp.exp(heights), extent[dim] // parts).reshape((-1,) + (1,) * (len(extent) - 1 - dim))
    return gain


def normal_values(key, shape, spread, bound, split=(), kind=jnp.bfloat16):
    array = jax.random.normal(key, shape, jnp.float32) * spread
    if len(split) > 0:
        array = block_levels(key, shape, split, -0.22, 0.18) * array
    return jnp.clip(array, min=-bound, max=bound).astype(kind)


def setup_inputs(seed: int = 0) -> dict:
    key_list = jax.random.split(jax.random.key(seed), 4)
    return {
        "mode_shapes": normal_values(key_list[0], (3, WINDOW, MODES), 1.0, 6.0, ((1, 8), (2, 128))),
        "mode_grads": normal_values(key_list[1], (8, WINDOW, MODES), 1.0, 6.0, ((1, 8), (2, 16))),
        "cell_weights": jnp.clip(jnp.exp(math.log(0.03) - 1.7917595 * jax.random.uniform(key_list[2], (WINDOW,), jnp.float32) ** block_levels(key_list[2], (WINDOW,), ((0, 8),), -0.2, 0.2)), 0.005, 0.03),
    }


def full_gradient(grad_piece):
    values = grad_piece.astype(jnp.float32)
    last = -(values[0] + values[4])
    return jnp.concatenate([values, last[None]], axis=0)


def convect_terms(shape_cols, grad_piece, weights):
    gradient = full_gradient(grad_piece)
    columns = shape_cols.astype(jnp.float32)
    rows_list = []
    for comp in range(3):
        total = columns[0][:, :, None] * gradient[comp * 3][:, None, :]
        total = total + columns[1][:, :, None] * gradient[comp * 3 + 1][:, None, :]
        total = total + columns[2][:, :, None] * gradient[comp * 3 + 2][:, None, :]
        rows_list.append(total * weights[:, None, None])
    return jnp.stack(rows_list, axis=0).astype(jnp.bfloat16)


def reference(mode_shapes, mode_grads, cell_weights):
    width_block = 64
    shapes_blocks = mode_shapes.reshape(3, N_SPACE, CELLS_DEV, MODES).transpose(1, 0, 2, 3)
    grads_blocks = mode_grads.reshape(8, N_SPACE, CELLS_DEV, MODES).transpose(1, 0, 2, 3)
    weight_blocks = cell_weights.reshape(N_SPACE, CELLS_DEV)

    def one_block(accum, inputs):
        shapes_here, grads_here, weights_here = inputs
        left = shapes_here.reshape(3 * CELLS_DEV, MODES).astype(jnp.float32)

        def one_group(group):
            grad_piece = lax.dynamic_slice_in_dim(grads_here, (group * width_block).astype(jnp.int32), width_block, 2)
            convect = convect_terms(shapes_here, grad_piece, weights_here)
            right = convect.reshape(3 * CELLS_DEV, MODES * width_block).astype(jnp.float32)
            product = lax.dot_general(left, right, (((0,), (0,)), ((), ())), preferred_element_type=jnp.float32)
            return product.reshape(MODES, MODES, width_block).astype(jnp.bfloat16)

        groups = lax.map(one_group, jnp.arange(MODES // width_block, dtype=jnp.int32))
        partial_sum = groups.transpose(1, 2, 0, 3).reshape(MODES, MODES, MODES)
        return accum + partial_sum.astype(jnp.float32), None

    start = jnp.zeros((MODES, MODES, MODES), jnp.float32)
    total, unused = lax.scan(one_block, start, (shapes_blocks, grads_blocks, weight_blocks))
    return total.astype(jnp.bfloat16)
```

```python
import functools

import jax
import jax.numpy as jnp
from jax import lax
from jax.experimental import pallas as pl
from jax.experimental.pallas import tpu as pltpu
from jax.sharding import PartitionSpec as P

MESH = pl.DeviceIdType.MESH
BF = jnp.bfloat16
F32 = jnp.float32
LANES = 128
NT = (((1,), (1,)), ((), ()))


def kernel(
    n,
    phi_ref,
    grad_ref,
    weight_ref,
    out_ref,
    own_phi,
    grads,
    second,
    first,
    left,
    right,
    sent,
    landed,
    tidy,
    send,
    recv_i1,
    recv_j1,
    recv_i2,
    recv_j2,
    recv_im,
    recv_jm,
    recv_g,
    recv_o,
    ready,
):
    y = lax.axis_index("space")
    z = lax.axis_index("modej")
    mk = lax.axis_index("modek")
    x = mk // 2
    c = mk % 2
    half = n // 2

    def at(yy, zz, xx, cc):
        return (yy, zz, xx * 2 + cc)

    def step(v, d):
        return lax.rem(v + d, n)

    def remote(src, dst, ssem, rsem, dev):
        return pltpu.make_async_remote_copy(
            src_ref=src, dst_ref=dst, send_sem=ssem, recv_sem=rsem, device_id=dev, device_id_type=MESH
        )

    def took(ref, sem):
        pltpu.make_async_copy(ref, ref, sem).wait()

    barrier = pltpu.get_barrier_semaphore()

    def hello(dev):
        pl.semaphore_signal(barrier, inc=1, device_id=dev, device_id_type=MESH)

    for d in range(1, n):
        hello(at(step(y, d), z, x, c))
        hello(at(step(y, d), z, x, 1 - c))
        hello(at(y, z, step(x, d), c))
        hello(at(y, step(z, d), x, c))
    hello(at(y, z, x, 1 - c))
    for t in range(n):
        @pl.when(jnp.logical_not((x == z) & (y == t)))
        def _():
            hello(at(t, x, z, c))

        @pl.when(jnp.logical_not((x == y) & (y == t)))
        def _():
            hello(at(t, z, y, c))

    rows = [jnp.transpose(phi_ref[a].astype(F32), (1, 0)) for a in range(3)]
    rows.append(jnp.zeros((4, LANES), F32))
    own_phi[...] = jnp.concatenate(rows, axis=0).astype(BF)
    weight = weight_ref[...]
    for ab in range(8):
        piece = jnp.transpose(grad_ref[ab].astype(F32), (1, 0)) * weight
        grads[y, ab * 32 : ab * 32 + 32, :] = piece.astype(BF)

    same_xz = (x == z).astype(jnp.int32)
    same_xy = (x == y).astype(jnp.int32)
    pl.semaphore_wait(barrier, 4 * (n - 1) + 1 + 2 * n - same_xz - same_xy)

    for d in range(1, n):
        pl.semaphore_signal(ready, inc=1, device_id=at(y, z, step(x, d), c), device_id_type=MESH)

    for t in range(n):
        self_i = (x == y) & (x == t)

        @pl.when(self_i)
        def _():
            pltpu.make_async_copy(own_phi, first.at[c, z, y], recv_i1).start()

        @pl.when(jnp.logical_not(self_i))
        def _():
            remote(own_phi, first.at[c, z, y], send.at[0], recv_i1, at(x, z, t, c)).start()

        self_j = (x == z) & (y == t)

        @pl.when(self_j)
        def _():
            pltpu.make_async_copy(own_phi, second.at[c, z, y], recv_j1).start()

        @pl.when(jnp.logical_not(self_j))
        def _():
            remote(own_phi, second.at[c, z, y], send.at[1], recv_j1, at(t, x, z, c)).start()

    for d in range(1, n):
        remote(grads.at[y], grads.at[y], send.at[6], recv_g.at[y], at(step(y, d), z, x, c)).start()

    took(first.at[c, z], recv_i1)
    for d in range(1, n):
        remote(first.at[c, z], first.at[c, z], send.at[2], recv_i2.at[z], at(y, step(z, d), x, c)).start()
    remote(first.at[c, z], first.at[c, z], send.at[4], recv_im.at[z], at(y, z, x, 1 - c)).start()
    took(second.at[c, x], recv_j1)
    for d in range(1, n):
        remote(second.at[c, x], second.at[c, x], send.at[3], recv_j2.at[x], at(y, z, step(x, d), c)).start()
    remote(second.at[c, x], second.at[c, x], send.at[5], recv_jm.at[x], at(y, z, x, 1 - c)).start()

    def turn(t):
        return lax.rem(jnp.where(t % 2 == 1, (t + 1) // 2, n - t // 2), n)

    def pass_i(t, carry):
        zs = step(z, turn(t))
        took(first.at[c, zs], recv_i2.at[zs])
        remote(first.at[c, zs], first.at[c, zs], send.at[4], recv_im.at[zs], at(y, z, x, 1 - c)).start()
        return carry

    lax.fori_loop(1, n, pass_i, 0)

    row_of = lax.broadcasted_iota(jnp.int32, (16, LANES), 0) // 4
    picks = [jnp.where(row_of == a, 1.0, 0.0).astype(BF) for a in range(3)]

    def build(t, carry):
        zs = step(z, turn(t))
        took(first.at[1 - c, zs], recv_im.at[zs])
        for cs in range(2):
            for ys in range(n):
                block = first[cs, zs, ys]
                for a in range(3):
                    at_row = pl.multiple_of(zs * 32 + cs * 16, 16)
                    left[pl.ds(at_row, 16), (ys * 3 + a) * LANES : (ys * 3 + a + 1) * LANES] = block * picks[a]
        return carry

    lax.fori_loop(0, n, build, 0)

    def await_g(d, carry):
        ys = step(y, d)
        took(grads.at[ys], recv_g.at[ys])
        return carry

    lax.fori_loop(1, n, await_g, 0)
    pl.semaphore_wait(ready, n - 1)
    owner_core = y // half
    place = lax.rem(y, half)
    low = lax.broadcasted_iota(jnp.int32, (8, 256), 0) < 4

    def chunk(t, carry):
        zs = step(x, turn(t))

        @pl.when(t < n - 1)
        def _():
            zn = step(x, turn(t + 1))
            took(second.at[c, zn], recv_j2.at[zn])
            remote(second.at[c, zn], second.at[c, zn], send.at[5], recv_jm.at[zn], at(y, z, x, 1 - c)).start()

        took(second.at[1 - c, zs], recv_jm.at[zs])

        for ys in range(n):
            g = [grads[ys, ab * 32 : ab * 32 + 32, :] for ab in range(8)]
            g.append(-(g[0] + g[4]))
            for cs in range(2):
                values = second[cs, zs, ys].astype(F32)
                for r in range(4):
                    v = [
                        jnp.broadcast_to(values[b * 4 + r : b * 4 + r + 1], (32, LANES)).astype(BF)
                        for b in range(3)
                    ]
                    for a in range(3):
                        total = v[0] * g[3 * a] + v[1] * g[3 * a + 1] + v[2] * g[3 * a + 2]
                        right[
                            (cs * 4 + r) * 32 : (cs * 4 + r) * 32 + 32,
                            (ys * 3 + a) * LANES : (ys * 3 + a + 1) * LANES,
                        ] = total
        product = lax.dot_general(left[...], right[...], NT, preferred_element_type=F32)
        for xd in range(n):
            parts = []
            for cs in range(2):
                base = xd * 32 + cs * 16
                both = product[base : base + 8] + product[base + 8 : base + 16]
                parts.append(both + pltpu.roll(both, 4, 0))
            tile = jnp.where(low, parts[0], parts[1])
            tile = jnp.concatenate([tile[:, :LANES], tile[:, LANES:]], axis=0)
            slot = zs * n + xd
            sent[slot] = tile.astype(BF)
            mine = (zs == y) & (x == xd) & (owner_core == c)

            @pl.when(mine)
            def _():
                pltpu.make_async_copy(sent.at[slot], landed.at[x, place, c], recv_o).start()

            @pl.when(jnp.logical_not(mine))
            def _():
                remote(
                    sent.at[slot], landed.at[x, place, c], send.at[7], recv_o, at(zs, z, xd, owner_core)
                ).start()
        return carry

    lax.fori_loop(0, n, chunk, 0)

    @pl.when(same_xy == 1)
    def _():
        took(first.at[0, 0, pl.ds(0, n - 1)], send.at[0])

    @pl.when(same_xy == 0)
    def _():
        took(first.at[0, 0], send.at[0])

    @pl.when(same_xz == 1)
    def _():
        took(second.at[0, 0, pl.ds(0, n - 1)], send.at[1])

    @pl.when(same_xz == 0)
    def _():
        took(second.at[0, 0], send.at[1])

    took(first.at[0, pl.ds(0, n - 1)], send.at[2])
    took(second.at[0, pl.ds(0, n - 1)], send.at[3])
    took(first.at[0], send.at[4])
    took(second.at[0], send.at[5])
    took(grads.at[pl.ds(0, n - 1)], send.at[6])

    @pl.when(owner_core == c)
    def _():
        took(sent.at[pl.ds(0, n * n - 1)], send.at[7])

    @pl.when(owner_core != c)
    def _():
        took(sent, send.at[7])

    took(landed, recv_o)

    lane = lax.broadcasted_iota(jnp.int32, (8, LANES), 1) // 32
    for p in range(half):
        for q in range(half):
            got = [landed[2 * q + s // 2, p, s % 2].astype(F32) for s in range(4)]
            for h in range(2):
                pieces = [g[h * 8 : h * 8 + 8] for g in got]
                for jl in range(4):
                    tile = pieces[jl]
                    for s in range(4):
                        if s != jl:
                            tile = jnp.where(lane == s, pltpu.roll(pieces[s], ((s - jl) * 32) % LANES, 1), tile)
                    tidy[q, pl.ds(p * 64 + h * 4 + jl, 8, stride=8), :] = tile
    for i in range(4 * n):
        for q in range(half):
            out_ref[i, :, q * LANES : (q + 1) * LANES] = tidy[q, i * 8 : i * 8 + 8, :].astype(BF)


def body(n, mode_shapes, mode_grads, cell_weights):
    vmem = pl.BlockSpec(memory_space=pltpu.VMEM)
    dma = pltpu.SemaphoreType.DMA
    return pl.pallas_call(
        functools.partial(kernel, n),
        out_shape=jax.ShapeDtypeStruct((4 * n, 8, 64 * n), BF),
        in_specs=[vmem] * 3,
        out_specs=vmem,
        scratch_shapes=[
            pltpu.VMEM((16, LANES), BF),
            pltpu.VMEM((n, 256, LANES), BF),
            pltpu.VMEM((2, n, n, 16, LANES), BF),
            pltpu.VMEM((2, n, n, 16, LANES), BF),
            pltpu.VMEM((32 * n, 3 * n * LANES), BF),
            pltpu.VMEM((256, 3 * n * LANES), BF),
            pltpu.VMEM((n * n, 16, LANES), BF),
            pltpu.VMEM((n, n // 2, 2, 16, LANES), BF),
            pltpu.VMEM((n // 2, 32 * n, LANES), F32),
            dma((8,)),
            dma(()),
            dma(()),
            dma((n,)),
            dma((n,)),
            dma((n,)),
            dma((n,)),
            dma((n,)),
            dma(()),
            pltpu.SemaphoreType.REGULAR,
        ],
        compiler_params=pltpu.CompilerParams(
            collective_id=0, has_side_effects=True, vmem_limit_bytes=40 * 2**20
        ),
    )(mode_shapes, mode_grads, cell_weights.reshape(1, -1))


def solution(mesh):
    n = mesh.shape["space"]
    in_specs = (P(None, "space", ("modej", "modek")), P(None, "space", "modek"), P("space"))
    out_specs = P("modek", ("space", "modej"), None)
    return jax.shard_map(
        functools.partial(body, n), mesh=mesh, in_specs=in_specs, out_specs=out_specs, check_vma=False
    )
```

```python
import functools

import jax
import jax.numpy as jnp
from jax import lax
from jax.experimental import pallas as pl
from jax.experimental.pallas import tpu as pltpu
from jax.sharding import PartitionSpec as P

MESH = pl.DeviceIdType.MESH
BF = jnp.bfloat16
F32 = jnp.float32
LANES = 128
NT = (((1,), (1,)), ((), ()))


def kernel(
    n,
    phi_hbm,
    grad_hbm,
    weight_hbm,
    out_ref,
    phi_ref,
    grad_ref,
    weight_ref,
    own_phi,
    grads,
    came_i,
    came_j,
    first,
    second,
    left,
    right,
    sent,
    landed,
    tidy,
    local,
    send,
    recv_i1,
    recv_j1,
    recv_i2,
    recv_j2,
    recv_im,
    recv_jm,
    recv_g,
    recv_o,
    ready,
):
    y = lax.axis_index("space")
    z = lax.axis_index("modej")
    mk = lax.axis_index("modek")
    x = mk // 2
    c = mk % 2
    half = n // 2
    tiles = 3 * n // 4

    def at(yy, zz, xx, cc):
        return (yy, zz, xx * 2 + cc)

    def step(v, d):
        return lax.rem(v + d, n)

    def remote(src, dst, ssem, rsem, dev):
        return pltpu.make_async_remote_copy(
            src_ref=src, dst_ref=dst, send_sem=ssem, recv_sem=rsem, device_id=dev, device_id_type=MESH
        )

    def took(ref, sem):
        pltpu.make_async_copy(ref, ref, sem).wait()

    mate = at(y, z, x, 1 - c)
    far_first = [half] + [d for k in range(half - 1, 0, -1) for d in (k, n - k)]
    opposite = lax.rem(2 * n - x - z, n)
    j_self = (x == 0) & (z == 0)
    i_self = x == y

    loads = [
        pltpu.make_async_copy(phi_hbm, phi_ref, local.at[0]),
        pltpu.make_async_copy(grad_hbm, grad_ref, local.at[1]),
        pltpu.make_async_copy(weight_hbm, weight_ref, local.at[2]),
    ]
    for load in loads:
        load.start()

    barrier = pltpu.get_barrier_semaphore()

    def hello(dev):
        pl.semaphore_signal(barrier, inc=1, device_id=dev, device_id_type=MESH)

    for d in far_first:
        @pl.when(jnp.logical_not(j_self))
        def _():
            hello(at(step(y, d), opposite, z, c))

        hello(at(step(y, d), z, y, c))
        hello(at(step(y, d), z, x, c))
        hello(at(step(y, d), z, x, 1 - c))
        hello(at(y, z, step(x, d), c))
        hello(at(y, step(z, d), x, c))

        @pl.when(j_self)
        def _():
            hello(at(step(y, d), opposite, z, c))

    @pl.when(jnp.logical_not(j_self))
    def _():
        hello(at(y, opposite, z, c))

    @pl.when(jnp.logical_not(i_self))
    def _():
        hello(at(y, z, y, c))

    hello(mate)

    for load in loads:
        load.wait()
    rows = [phi_ref[a].astype(F32) for a in range(3)]
    rows.append(jnp.zeros((4, LANES), F32))
    own_phi[...] = jnp.concatenate(rows, axis=0).astype(BF)
    weight = weight_ref[...]
    for ab in range(8):
        grads[y, ab * 32 : ab * 32 + 32, :] = (grad_ref[ab].astype(F32) * weight).astype(BF)

    pl.semaphore_wait(
        barrier, 4 * (n - 1) + 1 + 2 * n - j_self.astype(jnp.int32) - i_self.astype(jnp.int32)
    )

    for d in far_first:
        remote(own_phi, came_i.at[y], send.at[0], recv_i1, at(x, z, step(x, d), c)).start()

    @pl.when(i_self)
    def _():
        pltpu.make_async_copy(own_phi, came_i.at[y], recv_i1).start()

    @pl.when(jnp.logical_not(i_self))
    def _():
        remote(own_phi, came_i.at[y], send.at[0], recv_i1, at(x, z, x, c)).start()

    for d in far_first:
        remote(own_phi, came_j.at[y], send.at[1], recv_j1, at(step(y, d), x, opposite, c)).start()

    @pl.when(j_self)
    def _():
        pltpu.make_async_copy(own_phi, came_j.at[y], recv_j1).start()

    @pl.when(jnp.logical_not(j_self))
    def _():
        remote(own_phi, came_j.at[y], send.at[1], recv_j1, at(y, x, opposite, c)).start()

    for d in far_first:
        remote(grads.at[y], grads.at[y], send.at[6], recv_g.at[y], at(step(y, d), z, x, c)).start()
    for d in far_first:
        pl.semaphore_signal(ready, inc=1, device_id=at(y, z, step(x, d), c), device_id_type=MESH)

    row = lax.broadcasted_iota(jnp.int32, (16, LANES), 0)
    picks = [jnp.where(row // 4 == a, 1.0, 0.0).astype(BF) for a in range(4)]

    def pack(blocks, out):
        for t in range(tiles):
            moved = pltpu.roll(blocks[tiles + t // 3].astype(F32), (12 - 4 * (t % 3)) % 16, 0)
            out[t] = jnp.where(row < 12, blocks[t].astype(F32), moved).astype(BF)

    def spot(ys, a):
        return (ys, a) if ys < tiles else (3 * (ys - tiles) + a, 3)

    def build(zs, cs):
        at_row = pl.multiple_of(zs * 32 + cs * 16, 16)
        for ys in range(n):
            for a in range(3):
                t, group = spot(ys, a)
                left[pl.ds(at_row, 16), (ys * 3 + a) * LANES : (ys * 3 + a + 1) * LANES] = (
                    first[cs, zs, t] * picks[group]
                )

    def pass_i(d):
        zs = step(z, d)
        took(first.at[c, zs], recv_i2.at[zs])
        remote(first.at[c, zs], first.at[c, zs], send.at[4], recv_im.at[zs], mate).start()
        build(zs, c)

    def pass_j(xs):
        took(second.at[c, xs], recv_j2.at[xs])
        remote(second.at[c, xs], second.at[c, xs], send.at[5], recv_jm.at[xs], mate).start()

    def form(xs):
        for ys in range(n):
            g = [grads[ys, ab * 32 : ab * 32 + 32, :] for ab in range(8)]
            g.append(-(g[0] + g[4]))
            for cs in range(2):
                values = [second[cs, xs, spot(ys, b)[0]] for b in range(3)]
                for r in range(4):
                    v = []
                    for b in range(3):
                        at_r = spot(ys, b)[1] * 4 + r
                        v.append(jnp.broadcast_to(values[b][at_r : at_r + 1], (32, LANES)))
                    for a in range(3):
                        right[
                            (cs * 4 + r) * 32 : (cs * 4 + r) * 32 + 32,
                            (ys * 3 + a) * LANES : (ys * 3 + a + 1) * LANES,
                        ] = v[0] * g[3 * a] + v[1] * g[3 * a + 1] + v[2] * g[3 * a + 2]

    took(came_i, recv_i1)
    pack(came_i, first.at[c, z])
    for d in far_first:
        remote(first.at[c, z], first.at[c, z], send.at[2], recv_i2.at[z], at(y, step(z, d), x, c)).start()
    remote(first.at[c, z], first.at[c, z], send.at[4], recv_im.at[z], mate).start()
    build(z, c)
    took(came_j, recv_j1)
    pack(came_j, second.at[c, x])
    for d in far_first:
        remote(second.at[c, x], second.at[c, x], send.at[3], recv_j2.at[x], at(y, z, step(x, d), c)).start()
    remote(second.at[c, x], second.at[c, x], send.at[5], recv_jm.at[x], mate).start()

    def turn(t):
        return lax.rem(jnp.where(t % 2 == 1, (t + 1) // 2, n - t // 2), n)

    def pass_all(t, carry):
        pass_i(turn(t))
        return carry

    def build_mate(t, carry):
        zs = step(z, turn(t))
        took(first.at[1 - c, zs], recv_im.at[zs])
        build(zs, 1 - c)
        return carry

    def await_g(d, carry):
        ys = step(y, d)
        took(grads.at[ys], recv_g.at[ys])
        return carry

    def rank(dy):
        return jnp.where(dy >= half, 2 * (dy - half), 2 * (half - dy) - 1)

    own_rank = rank(lax.rem(opposite - y + n, n))

    def owner(t):
        u = jnp.where(t == 0, own_rank, jnp.where(t - 1 >= own_rank, t, t - 1))
        return lax.rem(y + jnp.where(u % 2 == 0, half + u // 2, half - (u + 1) // 2), n)

    def holder(zs):
        return lax.rem(2 * n - z - zs, n)

    lax.fori_loop(1, n, pass_all, 0)
    pass_j(holder(owner(1)))
    lax.fori_loop(1, n, await_g, 0)
    took(second.at[1 - c, x], recv_jm.at[x])
    form(x)
    lax.fori_loop(0, n, build_mate, 0)
    pl.semaphore_wait(ready, n - 1)
    owner_core = y // half
    place = lax.rem(y, half)
    low = lax.broadcasted_iota(jnp.int32, (8, 256), 0) < 4

    def chunk(t, carry):
        zs = owner(t)
        product = lax.dot_general(left[...], right[...], NT, preferred_element_type=F32)
        for xd in range(n):
            parts = []
            for cs in range(2):
                base = xd * 32 + cs * 16
                both = product[base : base + 8] + product[base + 8 : base + 16]
                parts.append(both + pltpu.roll(both, 4, 0))
            tile = jnp.where(low, parts[0], parts[1])
            tile = jnp.concatenate([tile[:, :LANES], tile[:, LANES:]], axis=0)
            sent[zs * n + xd] = tile.astype(BF)
        for d in far_first:
            xd = step(x, d)
            remote(
                sent.at[zs * n + xd], landed.at[x, place, c], send.at[7], recv_o, at(zs, z, xd, owner_core)
            ).start()
        mine = (zs == y) & (owner_core == c)

        @pl.when(mine)
        def _():
            pltpu.make_async_copy(sent.at[zs * n + x], landed.at[x, place, c], recv_o).start()

        @pl.when(jnp.logical_not(mine))
        def _():
            remote(
                sent.at[zs * n + x], landed.at[x, place, c], send.at[7], recv_o, at(zs, z, x, owner_core)
            ).start()

        @pl.when(t + 2 < n)
        def _():
            pass_j(holder(owner(t + 2)))

        @pl.when(t + 1 < n)
        def _():
            xs = holder(owner(t + 1))
            took(second.at[1 - c, xs], recv_jm.at[xs])
            form(xs)

        return carry

    lax.fori_loop(0, n, chunk, 0)

    took(landed, recv_o)

    lane = lax.broadcasted_iota(jnp.int32, (8, LANES), 1) // 32
    for p in range(half):
        for q in range(half):
            got = [landed[2 * q + s // 2, p, s % 2].astype(F32) for s in range(4)]
            for h in range(2):
                pieces = [g[h * 8 : h * 8 + 8] for g in got]
                for jl in range(4):
                    tile = pieces[jl]
                    for s in range(4):
                        if s != jl:
                            tile = jnp.where(lane == s, pltpu.roll(pieces[s], ((s - jl) * 32) % LANES, 1), tile)
                    tidy[q, pl.ds(p * 64 + h * 4 + jl, 8, stride=8), :] = tile
    for i in range(4 * n):
        for q in range(half):
            out_ref[i, :, q * LANES : (q + 1) * LANES] = tidy[q, i * 8 : i * 8 + 8, :].astype(BF)

    def left_by(flag, whole, less, sem):
        @pl.when(flag)
        def _():
            took(less, sem)

        @pl.when(jnp.logical_not(flag))
        def _():
            took(whole, sem)

    left_by(i_self, came_i, came_i.at[pl.ds(0, n - 1)], send.at[0])
    left_by(j_self, came_j, came_j.at[pl.ds(0, n - 1)], send.at[1])
    took(first.at[0, pl.ds(0, n - 1)], send.at[2])
    took(second.at[0, pl.ds(0, n - 1)], send.at[3])
    took(first.at[0], send.at[4])
    took(second.at[0], send.at[5])
    took(grads.at[pl.ds(0, n - 1)], send.at[6])
    left_by(owner_core == c, sent, sent.at[pl.ds(0, n * n - 1)], send.at[7])


def body(n, mode_shapes, mode_grads, cell_weights):
    dma = pltpu.SemaphoreType.DMA
    tiles = 3 * n // 4
    return pl.pallas_call(
        functools.partial(kernel, n),
        out_shape=jax.ShapeDtypeStruct((4 * n, 8, 64 * n), BF),
        in_specs=[pl.BlockSpec(memory_space=pl.ANY)] * 3,
        out_specs=pl.BlockSpec(memory_space=pltpu.VMEM),
        scratch_shapes=[
            pltpu.VMEM((3, 4, LANES), BF),
            pltpu.VMEM((8, 32, LANES), BF),
            pltpu.VMEM((1, LANES), F32),
            pltpu.VMEM((16, LANES), BF),
            pltpu.VMEM((n, 256, LANES), BF),
            pltpu.VMEM((n, 16, LANES), BF),
            pltpu.VMEM((n, 16, LANES), BF),
            pltpu.VMEM((2, n, tiles, 16, LANES), BF),
            pltpu.VMEM((2, n, tiles, 16, LANES), BF),
            pltpu.VMEM((32 * n, 3 * n * LANES), BF),
            pltpu.VMEM((256, 3 * n * LANES), BF),
            pltpu.VMEM((n * n, 16, LANES), BF),
            pltpu.VMEM((n, n // 2, 2, 16, LANES), BF),
            pltpu.VMEM((n // 2, 32 * n, LANES), F32),
            dma((3,)),
            dma((8,)),
            dma(()),
            dma(()),
            dma((n,)),
            dma((n,)),
            dma((n,)),
            dma((n,)),
            dma((n,)),
            dma(()),
            pltpu.SemaphoreType.REGULAR,
        ],
        compiler_params=pltpu.CompilerParams(
            collective_id=0, has_side_effects=True, vmem_limit_bytes=56 * 2**20
        ),
    )(
        jnp.transpose(mode_shapes, (0, 2, 1)),
        jnp.transpose(mode_grads, (0, 2, 1)),
        cell_weights.reshape(1, -1),
    )


def solution(mesh):
    n = mesh.shape["space"]
    in_specs = (P(None, "space", ("modej", "modek")), P(None, "space", "modek"), P("space"))
    out_specs = P("modek", ("space", "modej"), None)
    return jax.shard_map(
        functools.partial(body, n), mesh=mesh, in_specs=in_specs, out_specs=out_specs, check_vma=False
    )
```

```python
import functools

import jax
import jax.numpy as jnp
from jax import lax
from jax.experimental import pallas as pl
from jax.experimental.pallas import tpu as pltpu
from jax.sharding import PartitionSpec as P

MESH = pl.DeviceIdType.MESH
BF = jnp.bfloat16
F32 = jnp.float32
LANES = 128
NT = (((1,), (1,)), ((), ()))


def kernel(
    n,
    phi_hbm,
    grad_hbm,
    weight_hbm,
    landed,
    phi_ref,
    grad_ref,
    weight_ref,
    own_phi,
    grads,
    came_i,
    came_j,
    first,
    second,
    left,
    right,
    sent,
    local,
    send,
    recv_i1,
    recv_j1,
    recv_i2,
    recv_j2,
    recv_im,
    recv_jm,
    recv_g,
    recv_o,
    ready,
):
    y = lax.axis_index("space")
    z = lax.axis_index("modej")
    mk = lax.axis_index("modek")
    x = mk // 2
    c = mk % 2
    half = n // 2
    per = (3 * half + 3) // 4

    def at(yy, zz, xx, cc):
        return (yy, zz, xx * 2 + cc)

    def step(v, d):
        return lax.rem(v + d, n)

    def remote(src, dst, ssem, rsem, dev):
        return pltpu.make_async_remote_copy(
            src_ref=src, dst_ref=dst, send_sem=ssem, recv_sem=rsem, device_id=dev, device_id_type=MESH
        )

    def took(ref, sem):
        pltpu.make_async_copy(ref, ref, sem).wait()

    mate = at(y, z, x, 1 - c)
    far_first = [half] + [d for k in range(half - 1, 0, -1) for d in (k, n - k)]
    near_first = far_first[::-1]
    members = [[(g * half - n // 4 + k) % n for k in range(half)] for g in range(2)]
    group = lax.rem(y + n // 4, n) // half
    opposite = lax.rem(2 * n - x - z, n)
    j_self = (x == 0) & (z == 0)
    i_self = x == y

    loads = [
        pltpu.make_async_copy(phi_hbm, phi_ref, local.at[0]),
        pltpu.make_async_copy(grad_hbm, grad_ref, local.at[1]),
        pltpu.make_async_copy(weight_hbm, weight_ref, local.at[2]),
    ]
    for load in loads:
        load.start()

    barrier = pltpu.get_barrier_semaphore()

    def hello(dev):
        pl.semaphore_signal(barrier, inc=1, device_id=dev, device_id_type=MESH)

    for d in far_first:
        hello(at(step(y, d), opposite, z, c))
    for d in far_first:
        hello(at(step(y, d), z, y, c))

    @pl.when(jnp.logical_not(j_self))
    def _():
        hello(at(y, opposite, z, c))

    @pl.when(jnp.logical_not(i_self))
    def _():
        hello(at(y, z, y, c))

    for d in far_first:
        hello(at(step(y, d), z, x, c))
        hello(at(y, z, step(x, d), c))
        hello(at(y, step(z, d), x, c))
    for d in far_first:
        hello(at(step(y, d), z, x, 1 - c))
    hello(mate)

    loads[0].wait()
    rows = [phi_ref[a].astype(F32) for a in range(3)]
    rows.append(jnp.zeros((4, LANES), F32))
    own_phi[...] = jnp.concatenate(rows, axis=0).astype(BF)

    pl.semaphore_wait(
        barrier, 4 * (n - 1) + 1 + 2 * n - j_self.astype(jnp.int32) - i_self.astype(jnp.int32)
    )

    for d in far_first:
        remote(own_phi, came_i.at[y], send.at[0], recv_i1.at[group], at(x, z, step(x, d), c)).start()

    @pl.when(i_self)
    def _():
        pltpu.make_async_copy(own_phi, came_i.at[y], recv_i1.at[group]).start()

    @pl.when(jnp.logical_not(i_self))
    def _():
        remote(own_phi, came_i.at[y], send.at[0], recv_i1.at[group], at(x, z, x, c)).start()

    for d in far_first:
        remote(own_phi, came_j.at[y], send.at[1], recv_j1.at[group], at(step(y, d), x, opposite, c)).start()

    @pl.when(j_self)
    def _():
        pltpu.make_async_copy(own_phi, came_j.at[y], recv_j1.at[group]).start()

    @pl.when(jnp.logical_not(j_self))
    def _():
        remote(own_phi, came_j.at[y], send.at[1], recv_j1.at[group], at(y, x, opposite, c)).start()

    loads[1].wait()
    loads[2].wait()
    weight = weight_ref[...]
    for ab in range(8):
        grads[y, ab * 32 : ab * 32 + 32, :] = (grad_ref[ab].astype(F32) * weight).astype(BF)

    for d in far_first:
        remote(grads.at[y], grads.at[y], send.at[6], recv_g.at[y], at(step(y, d), z, x, c)).start()
    for d in far_first:
        pl.semaphore_signal(ready, inc=1, device_id=at(y, z, step(x, d), c), device_id_type=MESH)

    row = lax.broadcasted_iota(jnp.int32, (16, LANES), 0)
    picks = [jnp.where(row // 4 == a, 1.0, 0.0).astype(BF) for a in range(4)]

    spots = {}
    for g in range(2):
        for k, ys in enumerate(members[g]):
            for a in range(3):
                if k < per:
                    spots[ys, a] = (per * g + k, a)
                else:
                    spots[ys, a] = (per * g + 3 * (k - per) + a, 3)

    def pack(blocks, out, g):
        for k in range(per):
            block = blocks[members[g][k]]
            if per < half:
                moved = pltpu.roll(blocks[members[g][per + k // 3]].astype(F32), (12 - 4 * (k % 3)) % 16, 0)
                block = jnp.where(row < 12, block.astype(F32), moved).astype(BF)
            out[per * g + k] = block

    def build(zs, cs):
        at_row = pl.multiple_of(zs * 32 + cs * 16, 16)
        for ys in range(n):
            for a in range(3):
                t, quad = spots[ys, a]
                left[pl.ds(at_row, 16), (ys * 3 + a) * LANES : (ys * 3 + a + 1) * LANES] = (
                    first[cs, zs, t] * picks[quad]
                )

    def part(ref, core, at_v, g):
        return ref.at[core, at_v, pl.ds(per * g, per)]

    def pass_i(zs):
        for g in range(2):
            block = part(first, c, zs, g)
            took(block, recv_i2.at[zs, g])
            remote(block, block, send.at[4], recv_im.at[zs, g], mate).start()
        build(zs, c)

    def pass_j(xs):
        for g in range(2):
            block = part(second, c, xs, g)
            took(block, recv_j2.at[xs, g])
            remote(block, block, send.at[5], recv_jm.at[xs, g], mate).start()

    def form(xs, await_block=None):
        for ys in range(n):
            if await_block is not None:
                await_block(ys)
            g = [grads[ys, ab * 32 : ab * 32 + 32, :] for ab in range(8)]
            g.append(-(g[0] + g[4]))
            for cs in range(2):
                values = [second[cs, xs, spots[ys, b][0]] for b in range(3)]
                for r in range(4):
                    v = []
                    for b in range(3):
                        at_r = spots[ys, b][1] * 4 + r
                        v.append(jnp.broadcast_to(values[b][at_r : at_r + 1], (32, LANES)))
                    for a in range(3):
                        right[
                            (cs * 4 + r) * 32 : (cs * 4 + r) * 32 + 32,
                            (ys * 3 + a) * LANES : (ys * 3 + a + 1) * LANES,
                        ] = v[0] * g[3 * a] + v[1] * g[3 * a + 1] + v[2] * g[3 * a + 2]

    for g in range(2):
        took(came_i.at[pl.ds(0, half)], recv_i1.at[g])
        pack(came_i, first.at[c, z], g)
        block = part(first, c, z, g)
        for d in near_first:
            remote(block, block, send.at[2], recv_i2.at[z, g], at(y, step(z, d), x, c)).start()
        remote(block, block, send.at[4], recv_im.at[z, g], mate).start()
        took(came_j.at[pl.ds(0, half)], recv_j1.at[g])
        pack(came_j, second.at[c, x], g)
        block = part(second, c, x, g)
        for d in near_first:
            remote(block, block, send.at[3], recv_j2.at[x, g], at(y, z, step(x, d), c)).start()
        remote(block, block, send.at[5], recv_jm.at[x, g], mate).start()
    build(z, c)

    def turn(t):
        return lax.rem(jnp.where(t % 2 == 1, (t + 1) // 2, n - t // 2), n)

    def build_mate(zs, carry):
        for g in range(2):
            took(part(first, 1 - c, zs, g), recv_im.at[zs, g])
        build(zs, 1 - c)
        return carry

    def await_g(ys):
        @pl.when(ys != y)
        def _():
            took(grads.at[ys], recv_g.at[ys])

    def rank(dy):
        return jnp.where(dy >= half, 2 * (dy - half), 2 * (half - dy) - 1)

    own_rank = rank(lax.rem(opposite - y + n, n))

    def owner(t):
        u = jnp.where(t == 0, own_rank, jnp.where(t - 1 >= own_rank, t, t - 1))
        return lax.rem(y + jnp.where(u % 2 == 0, half + u // 2, half - (u + 1) // 2), n)

    def holder(zs):
        return lax.rem(2 * n - z - zs, n)

    def pass_all(t, carry):
        pass_i(step(z, turn(t)))
        return carry

    lax.fori_loop(1, n, pass_all, 0)
    pass_j(holder(owner(1)))
    for g in range(2):
        took(part(second, 1 - c, x, g), recv_jm.at[x, g])
    form(x, await_g)
    lax.fori_loop(0, n, build_mate, 0)
    pl.semaphore_wait(ready, n - 1)
    owner_core = y // half
    place = lax.rem(y, half)
    low = lax.broadcasted_iota(jnp.int32, (8, 256), 0) < 4

    def chunk(t, carry):
        zs = owner(t)
        product = lax.dot_general(left[...], right[...], NT, preferred_element_type=F32)
        for xd in range(n):
            parts = []
            for cs in range(2):
                base = xd * 32 + cs * 16
                both = product[base : base + 8] + product[base + 8 : base + 16]
                parts.append(both + pltpu.roll(both, 4, 0))
            tile = jnp.where(low, parts[0], parts[1])
            tile = jnp.concatenate([tile[:, :LANES], tile[:, LANES:]], axis=0)
            sent[zs * n + xd] = tile.astype(BF)
        for d in far_first:
            xd = step(x, d)
            remote(
                sent.at[zs * n + xd], landed.at[x, place, c], send.at[7], recv_o, at(zs, z, xd, owner_core)
            ).start()
        mine = (zs == y) & (owner_core == c)

        @pl.when(mine)
        def _():
            pltpu.make_async_copy(sent.at[zs * n + x], landed.at[x, place, c], recv_o).start()

        @pl.when(jnp.logical_not(mine))
        def _():
            remote(
                sent.at[zs * n + x], landed.at[x, place, c], send.at[7], recv_o, at(zs, z, x, owner_core)
            ).start()

        @pl.when(t + 2 < n)
        def _():
            pass_j(holder(owner(t + 2)))

        @pl.when(t + 1 < n)
        def _():
            xs = holder(owner(t + 1))
            for g in range(2):
                took(part(second, 1 - c, xs, g), recv_jm.at[xs, g])
            form(xs)

        return carry

    lax.fori_loop(0, n, chunk, 0)

    took(landed, recv_o)

    def left_by(flag, whole, less, sem):
        @pl.when(flag)
        def _():
            took(less, sem)

        @pl.when(jnp.logical_not(flag))
        def _():
            took(whole, sem)

    left_by(i_self, came_i, came_i.at[pl.ds(0, n - 1)], send.at[0])
    left_by(j_self, came_j, came_j.at[pl.ds(0, n - 1)], send.at[1])
    took(first.at[0, pl.ds(0, n - 1)], send.at[2])
    took(second.at[0, pl.ds(0, n - 1)], send.at[3])
    took(first.at[0], send.at[4])
    took(second.at[0], send.at[5])
    took(grads.at[pl.ds(0, n - 1)], send.at[6])
    left_by(owner_core == c, sent, sent.at[pl.ds(0, n * n - 1)], send.at[7])


def arrange(n, landed, out_ref, tidy):
    half = n // 2
    lane = lax.broadcasted_iota(jnp.int32, (8, LANES), 1) // 32
    for p in range(half):
        for q in range(half):
            got = [landed[2 * q + s // 2, p, s % 2].astype(F32) for s in range(4)]
            for h in range(2):
                pieces = [g[h * 8 : h * 8 + 8] for g in got]
                for jl in range(4):
                    tile = pieces[jl]
                    for s in range(4):
                        if s != jl:
                            tile = jnp.where(lane == s, pltpu.roll(pieces[s], ((s - jl) * 32) % LANES, 1), tile)
                    tidy[q, pl.ds(p * 64 + h * 4 + jl, 8, stride=8), :] = tile
    for i in range(4 * n):
        for q in range(half):
            out_ref[i, :, q * LANES : (q + 1) * LANES] = tidy[q, i * 8 : i * 8 + 8, :].astype(BF)


def body(n, mode_shapes, mode_grads, cell_weights):
    dma = pltpu.SemaphoreType.DMA
    tiles = 2 * ((3 * (n // 2) + 3) // 4)
    parts = pl.pallas_call(
        functools.partial(kernel, n),
        out_shape=jax.ShapeDtypeStruct((n, n // 2, 2, 16, LANES), BF),
        in_specs=[pl.BlockSpec(memory_space=pl.ANY)] * 3,
        out_specs=pl.BlockSpec(memory_space=pl.ANY),
        scratch_shapes=[
            pltpu.VMEM((3, 4, LANES), BF),
            pltpu.VMEM((8, 32, LANES), BF),
            pltpu.VMEM((1, LANES), F32),
            pltpu.VMEM((16, LANES), BF),
            pltpu.VMEM((n, 256, LANES), BF),
            pltpu.VMEM((n, 16, LANES), BF),
            pltpu.VMEM((n, 16, LANES), BF),
            pltpu.VMEM((2, n, tiles, 16, LANES), BF),
            pltpu.VMEM((2, n, tiles, 16, LANES), BF),
            pltpu.VMEM((32 * n, 3 * n * LANES), BF),
            pltpu.VMEM((256, 3 * n * LANES), BF),
            pltpu.VMEM((n * n, 16, LANES), BF),
            dma((3,)),
            dma((8,)),
            dma((2,)),
            dma((2,)),
            dma((n, 2)),
            dma((n, 2)),
            dma((n, 2)),
            dma((n, 2)),
            dma((n,)),
            dma(()),
            pltpu.SemaphoreType.REGULAR,
        ],
        compiler_params=pltpu.CompilerParams(
            collective_id=0, has_side_effects=True, vmem_limit_bytes=56 * 2**20
        ),
    )(
        jnp.transpose(mode_shapes, (0, 2, 1)),
        jnp.transpose(mode_grads, (0, 2, 1)),
        cell_weights.reshape(1, -1),
    )
    return pl.pallas_call(
        functools.partial(arrange, n),
        out_shape=jax.ShapeDtypeStruct((4 * n, 8, 64 * n), BF),
        in_specs=[pl.BlockSpec(memory_space=pltpu.VMEM)],
        out_specs=pl.BlockSpec(memory_space=pltpu.VMEM),
        scratch_shapes=[pltpu.VMEM((n // 2, 32 * n, LANES), F32)],
    )(parts)


def solution(mesh):
    n = mesh.shape["space"]
    in_specs = (P(None, "space", ("modej", "modek")), P(None, "space", "modek"), P("space"))
    out_specs = P("modek", ("space", "modej"), None)
    return jax.shard_map(
        functools.partial(body, n), mesh=mesh, in_specs=in_specs, out_specs=out_specs, check_vma=False
    )
```
